32 devices in a mesh: row: 8 (over z, y), col: 4 (over x, core).
Axes of the slice: x: 2, y: 2, z: 4, core: 2. Of those that a mesh axis runs over, the one named last changes fastest.
Arguments:
- child_update: bfloat16 [32768, 16384], P('row', 'col'), may hold values from -6 to 6
- child_map: int32 [2, 128], replicated, may hold values from 0 to 191, as said below
- tile_mask: int32 [192, 192], replicated, may hold values 0 or 1
- diag_inverse: bfloat16 [768, 768], replicated, may hold values from -0.0078125 to 0.0078125
Outputs:
- factored: bfloat16 [24576, 24576], P('row', 'col')
The draws below stay inside these ranges and needn't reach their ends.
Inputs may be any that keep to these rules, and one draw needn't show every extreme that they name: Each row of child_map holds distinct parent blocks. Of each aligned run of 32 entries of a row, at most 4 lie in any one aligned run of 24 parent blocks, and every such run that is hit holds exactly 4; of each aligned run of 32 entries, at most 8 lie in any one aligned run of 48 parent blocks, and every run hit holds exactly 8.
All inputs are finite; a program needn't handle non-finite values.
Results may differ from the reference program's by a relative error of at most 0.0042.
Values may be sent and summed in bfloat16 or wider, within the bound.
A program may use at most 384 MiB of HBM per device.

```python
import jax
import jax.numpy as jnp
from jax import lax

CB = 128
NCB = 128
CU = 16384
NPB = 192
P_SIZE = 24576
PW = 768


def draw_child_map(key, part):
    key = jax.random.fold_in(key, 11)
    first, second, third = jax.random.split(key, 3)
    groups = NCB // 2
    sigma = jax.random.permutation(first, 8).astype(jnp.int32)
    tau = jax.random.permutation(second, 8).astype(jnp.int32)
    index = jnp.arange(groups, dtype=jnp.int32)
    target = 8 * sigma[index % 8] + tau[index // 8]
    scores = jax.random.randint(third, (groups, 3), 0, 1 << 20, dtype=jnp.int32) * 3 + jnp.arange(3, dtype=jnp.int32)[None, :]
    order = jnp.argsort(scores, axis=1, stable=True).astype(jnp.int32)
    parents = 3 * target[:, None] + order
    first_child = jnp.stack([parents[:, 0], parents[:, 1]], axis=1).reshape(NCB)
    second_child = jnp.stack([parents[:, 0], parents[:, 2]], axis=1).reshape(NCB)
    return jnp.stack([first_child, second_child]).astype(jnp.int32)


def touch_ends(entries, key, least, high):
    longest = entries.shape.index(max(entries.shape))
    spots = []
    for shift in (0, 1):
        where = [jax.random.randint(jax.random.fold_in(key, axis), (), 0, length) for axis, length in enumerate(entries.shape)]
        where[longest] = (where[longest] + shift) % entries.shape[longest]
        spots.append(tuple(where))
    return entries.at[spots[0]].set(least).at[spots[1]].set(high)


def levels(rng, dims, pieces, least, largest):
    gain = 1.0
    for position, parts in pieces:
        draws = jax.random.uniform(jax.random.fold_in(jax.random.fold_in(rng, 6), position), (parts,), jnp.float32, least / len(pieces), largest / len(pieces))
        gain = gain * jnp.repeat(jnp.exp(draws), dims[position] // parts).reshape((-1,) + (1,) * (len(dims) - 1 - position))
    return gain


def centred(rng, dims, deviation, bound, pieces=(), kind=jnp.bfloat16):
    values = jax.random.normal(rng, dims, jnp.float32) * deviation
    if len(pieces) > 0:
        values = levels(rng, dims, pieces, -0.22, 0.18) * values
    return jnp.clip(values, min=-bound, max=bound).astype(kind)


def setup_inputs(seed: int = 0) -> dict:
    key_of = jax.random.split(jax.random.key(seed), 5)
    child_update = centred(key_of[0], (2 * CU, CU), 1.0, 6.0, ((0, 8), (1, 4)))
    child_map = draw_child_map(jax.random.fold_in(key_of[4], 71), 0)
    tile_mask = touch_ends((jax.random.randint(key_of[2], (NPB, NPB), 0, 3) < 2).astype(jnp.int32), jax.random.fold_in(key_of[2], 1), 0, 1)
    diag_inverse = centred(key_of[3], (PW, PW), (PW * PW) ** -0.5, 0.0078125)
    return dict(child_update=child_update, child_map=child_map, tile_mask=tile_mask, diag_inverse=diag_inverse)


def reference(child_update, child_map, tile_mask, diag_inverse):
    blocks = child_update.reshape(2, NCB, CB, NCB, CB)
    whole = jnp.zeros((NPB, NPB, CB, CB), jnp.float32)
    for child in range(2):
        parents = child_map[child].astype(jnp.int32)
        tiles = blocks[child].transpose(0, 2, 1, 3).astype(jnp.float32)
        whole = whole.at[parents[:, None], parents[None, :]].add(tiles)
    front = whole.astype(jnp.bfloat16).transpose(0, 2, 1, 3).reshape(P_SIZE, P_SIZE)
    row_ids = jnp.arange(P_SIZE, dtype=jnp.int32)[:, None]
    lower = jnp.dot(front[:, :PW], diag_inverse, preferred_element_type=jnp.float32)
    lower = jnp.where(row_ids >= PW, lower, jnp.float32(0.0)).astype(jnp.bfloat16)
    upper = front[:PW, :]
    keep = tile_mask.astype(jnp.float32)
    col_ids = jnp.arange(P_SIZE, dtype=jnp.int32)[None, :]

    def one_block(items):
        lower_rows, front_rows, keep_row = items
        update = jnp.dot(lower_rows, upper, preferred_element_type=jnp.float32)
        update = (update.reshape(CB, NPB, CB) * keep_row[None, :, None]).reshape(CB, P_SIZE)
        schur = (front_rows.astype(jnp.float32) - update).astype(jnp.bfloat16)
        panel = jnp.where(jnp.sum(jnp.abs(lower_rows.astype(jnp.float32))) >= 0.0, lower_rows, lower_rows)
        return schur, panel

    schur, _ = lax.map(one_block, (lower.reshape(NPB, CB, PW), front.reshape(NPB, CB, P_SIZE), keep))
    schur = schur.reshape(P_SIZE, P_SIZE)
    left = jnp.where(row_ids >= PW, jnp.pad(lower, ((0, 0), (0, P_SIZE - PW))), front)
    return jnp.where(col_ids < PW, left, schur)
```

```python
import functools

import jax
import jax.numpy as jnp
from jax import lax
from jax.experimental import pallas as pl
from jax.experimental.pallas import tpu as pltpu
from jax.sharding import PartitionSpec as P

CB = 128
MESH = pl.DeviceIdType.MESH
VMEM_LIMIT = 56 * 1024 * 1024


def ranks(child_map, run, owned):
    count = child_map.shape[1]
    target = child_map // owned
    places = jnp.arange(count, dtype=jnp.int32)
    same = (target[:, :, None] == target[:, None, :]) & (
        (places[:, None] // run == places[None, :] // run) & (places[None, :] < places[:, None])
    )[None]
    return jnp.sum(same.astype(jnp.int32), axis=2)


def send_table(child_map, rank, child, start, run, owned, dests, cap):
    parents = lax.dynamic_slice(child_map, (child, start), (1, run))[0]
    rank = lax.dynamic_slice(rank, (child, start), (1, run))[0]
    slot = (parents // owned) * cap + rank
    hits = slot[None, :] == jnp.arange(dests * cap, dtype=jnp.int32)[:, None]
    return jnp.sum(jnp.where(hits, jnp.arange(run, dtype=jnp.int32)[None, :], 0), axis=1)


def receive_table(child_map, rank, mine, run, owned):
    count = child_map.shape[1]
    wanted = mine * owned + jnp.arange(owned, dtype=jnp.int32)
    hits = child_map[:, None, :] == wanted[None, :, None]
    shard = jnp.arange(count, dtype=jnp.int32) // run
    shard = jnp.sum(jnp.where(hits, shard[None, None, :], 0), axis=2)
    slot = jnp.sum(jnp.where(hits, rank[:, None, :], 0), axis=2)
    return shard, slot, jnp.any(hits, axis=2).astype(jnp.int32)


def pack_kernel(dests, slots, row_src, col_src, x_ref, o_ref):
    for c in range(dests):
        for t in range(slots):
            at = pl.multiple_of(col_src[c * slots + t] * CB, CB)
            o_ref[0, c, 0, :, t * CB : (t + 1) * CB] = x_ref[:, pl.ds(at, CB)]


def front_tile(tiles, flags, col_tab, own_cols, col):
    total = None
    for k in range(2):
        a = col_tab[(0 + k) * own_cols + col]
        t = pl.multiple_of(col_tab[(2 + k) * own_cols + col] * CB, CB)
        there = (flags[k] * col_tab[(4 + k) * own_cols + col]).astype(jnp.float32)
        part = tiles[k][0, a, 0, :, pl.ds(t, CB)].astype(jnp.float32) * there
        total = part if total is None else total + part
    return total.astype(jnp.bfloat16)


def row_flags(row_tab, own_rows, row):
    return [row_tab[(4 + k) * own_rows + row] for k in range(2)]


def upper_kernel(own_rows, own_cols, row_tab, col_tab, t0, t1, o_ref):
    flags = row_flags(row_tab, own_rows, pl.program_id(0))
    for j in range(own_cols):
        o_ref[:, j * CB : (j + 1) * CB] = front_tile((t0, t1), flags, col_tab, own_cols, j)


def lower_kernel(own_rows, own_cols, group, panel, row_tab, col_tab, place, *refs):
    tiles, (inv_ref, o_ref, held) = refs[: 2 * group], refs[2 * group :]
    for r in range(group):
        row = pl.program_id(0) * group + r
        flags = row_flags(row_tab, own_rows, row)
        for j in range(panel):
            held[r * CB : (r + 1) * CB, j * CB : (j + 1) * CB] = front_tile(
                tiles[2 * r : 2 * r + 2], flags, col_tab, own_cols, j
            )
    lower = jnp.dot(held[...], inv_ref[...], preferred_element_type=jnp.float32)
    for r in range(group):
        row = place[0] * own_rows + pl.program_id(0) * group + r
        below = (row >= panel).astype(jnp.float32)
        o_ref[r * CB : (r + 1) * CB, :] = (lower[r * CB : (r + 1) * CB] * below).astype(jnp.bfloat16)


def final_kernel(own_rows, own_cols, group, panel, wide, row_tab, col_tab, place, keep, *refs):
    tiles, (lower_ref, upper_ref, o_ref) = refs[: 2 * group], refs[2 * group :]
    rows = [pl.program_id(0) * group + r for r in range(group)]
    flags = [row_flags(row_tab, own_rows, row) for row in rows]

    def step(n, carry):
        at = pl.multiple_of(n * (wide * CB), wide * CB)
        update = jnp.dot(
            lower_ref[...], upper_ref[:, pl.ds(at, wide * CB)], preferred_element_type=jnp.float32
        )
        for q in range(wide):
            col = n * wide + q
            for r in range(group):
                front = front_tile(tiles[2 * r : 2 * r + 2], flags[r], col_tab, own_cols, col)
                mask = keep[rows[r] * own_cols + col].astype(jnp.float32)
                part = update[r * CB : (r + 1) * CB, q * CB : (q + 1) * CB] * mask
                o_ref[r * CB : (r + 1) * CB, pl.ds(pl.multiple_of(at + q * CB, CB), CB)] = (
                    front.astype(jnp.float32) - part
                ).astype(jnp.bfloat16)
        return carry

    lax.fori_loop(0, own_cols // wide, step, 0)
    for r in range(group):

        @pl.when((place[1] == 0) & (place[0] * own_rows + rows[r] >= panel))
        def _():
            o_ref[r * CB : (r + 1) * CB, : panel * CB] = lower_ref[r * CB : (r + 1) * CB, :]


def spread_kernel(n, m, chunks, u_in, l_in, upper, lower, down, across, first, line, other, l_send, l_recv):
    row, col = lax.axis_index("row"), lax.axis_index("col")
    high, low = row // 2, row % 2
    barrier = pltpu.get_barrier_semaphore()
    for off in range(1, n):
        pl.semaphore_signal(barrier, inc=1, device_id=(lax.rem(row + off, n), col), device_id_type=MESH)
    for off in range(1, m):
        pl.semaphore_signal(barrier, inc=1, device_id=(row, lax.rem(col + off, m)), device_id_type=MESH)
    pl.semaphore_wait(barrier, n + m - 2)

    depth = upper.shape[0] // (2 * chunks)
    root = row == 0
    partner = high * 2 + (1 - low)
    goes_down = row + 2 < n
    goes_across = row != 1

    def move(half, c, send, recv, to):
        at = pl.multiple_of((half * chunks + c) * depth, depth)
        part = upper.at[pl.ds(at, depth), :]
        return pltpu.make_async_remote_copy(
            src_ref=part, dst_ref=part, send_sem=send.at[c], recv_sem=recv.at[c],
            device_id=(to, col), device_id_type=MESH,
        )

    def move_lower(p):
        return pltpu.make_async_remote_copy(
            src_ref=lower, dst_ref=lower, send_sem=l_send.at[p - 1], recv_sem=l_recv,
            device_id=(row, p), device_id_type=MESH,
        )

    for p in range(m - 1, 0, -1):

        @pl.when(col == 0)
        def _():
            move_lower(p).start()

    def send(c, carry):
        @pl.when(row != 0)
        def _():
            move(low, c, down, line, partner).wait_recv()

        @pl.when(goes_down)
        def _():
            move(low, c, down, line, row + 2).start()

        @pl.when(root)
        def _():
            move(1, c, first, line, 1).start()

        @pl.when(goes_across)
        def _():
            move(low, c, across, other, partner).start()

        return carry

    lax.fori_loop(0, chunks, send, 0)

    def finish(c, carry):
        @pl.when(row != 0)
        def _():
            move(1 - low, c, across, other, partner).wait_recv()

        @pl.when(goes_down)
        def _():
            move(low, c, down, line, row + 2).wait_send()

        @pl.when(root)
        def _():
            move(1, c, first, line, 1).wait_send()

        @pl.when(goes_across)
        def _():
            move(low, c, across, other, partner).wait_send()

        return carry

    lax.fori_loop(0, chunks, finish, 0)

    @pl.when(col != 0)
    def _():
        move_lower(1).wait_recv()

    for p in range(1, m):

        @pl.when(col == 0)
        def _():
            move_lower(p).wait_send()


def spread(upper, lower, n, m):
    chunks = 12
    dma = pltpu.SemaphoreType.DMA
    anywhere = pl.BlockSpec(memory_space=pl.ANY)
    return pl.pallas_call(
        functools.partial(spread_kernel, n, m, chunks),
        out_shape=(
            jax.ShapeDtypeStruct(upper.shape, upper.dtype),
            jax.ShapeDtypeStruct(lower.shape, lower.dtype),
        ),
        in_specs=[anywhere] * 2,
        out_specs=(anywhere, anywhere),
        scratch_shapes=[dma((chunks,))] * 5 + [dma((m - 1,)), dma],
        input_output_aliases={0: 0, 1: 1},
        compiler_params=pltpu.CompilerParams(collective_id=0, has_side_effects=True),
    )(upper, lower)


def body(child_update, child_map, tile_mask, diag_inverse):
    n, m = lax.axis_size("row"), lax.axis_size("col")
    row_index, col_index = lax.axis_index("row"), lax.axis_index("col")
    per_child = n // 2
    blocks = child_map.shape[1]
    row_blocks, col_blocks = child_update.shape[0] // CB, child_update.shape[1] // CB
    own_rows, own_cols = tile_mask.shape[0] // n, tile_mask.shape[1] // m
    width = diag_inverse.shape[0]
    panel = width // CB
    cap_rows = 2 * (16 // n) * max(1, 8 // n)
    cap_cols = blocks // (m * m)
    child, within = row_index // per_child, row_index % per_child

    row_rank = ranks(child_map, row_blocks, own_rows)
    col_rank = ranks(child_map, col_blocks, own_cols)
    row_src = send_table(child_map, row_rank, child, within * row_blocks, row_blocks, own_rows, n, cap_rows)
    col_src = send_table(child_map, col_rank, child, col_index * col_blocks, col_blocks, own_cols, m, cap_cols)
    shard, slot, there = receive_table(child_map, row_rank, row_index, row_blocks, own_rows)
    shard = shard + per_child * jnp.arange(2, dtype=jnp.int32)[:, None]
    row_tab = jnp.concatenate([shard, slot, there]).reshape(-1)
    col_tab = jnp.concatenate(receive_table(child_map, col_rank, col_index, col_blocks, own_cols)).reshape(-1)
    place = jnp.stack([row_index, col_index]).astype(jnp.int32)
    keep = lax.dynamic_slice(
        tile_mask, (row_index * own_rows, col_index * own_cols), (own_rows, own_cols)
    ).reshape(-1)

    params = pltpu.CompilerParams(vmem_limit_bytes=VMEM_LIMIT)
    tile_block = (1, m, 1, CB, cap_cols * CB)
    packed = pl.pallas_call(
        functools.partial(pack_kernel, m, cap_cols),
        grid_spec=pltpu.PrefetchScalarGridSpec(
            num_scalar_prefetch=2,
            grid=(n * cap_rows,),
            in_specs=[pl.BlockSpec((CB, col_blocks * CB), lambda g, rs, cs: (rs[g], 0))],
            out_specs=pl.BlockSpec(tile_block, lambda g, rs, cs: (g // cap_rows, 0, g % cap_rows, 0, 0)),
        ),
        out_shape=jax.ShapeDtypeStruct((n, m, cap_rows, CB, cap_cols * CB), jnp.bfloat16),
        compiler_params=params,
    )(row_src, col_src, child_update)
    arrived = lax.all_to_all(
        packed.reshape(n * m, cap_rows, CB, cap_cols * CB), ("row", "col"), split_axis=0, concat_axis=0, tiled=True
    ).reshape(packed.shape)

    def tile_specs(group):
        def spec(r, k):
            def where(g, row_tab, *_):
                row = g * group + r
                return (row_tab[k * own_rows + row], 0, row_tab[(2 + k) * own_rows + row], 0, 0)

            return pl.BlockSpec(tile_block, where)

        return [spec(r, k) for r in range(group) for k in range(2)]

    upper = pl.pallas_call(
        functools.partial(upper_kernel, own_rows, own_cols),
        grid_spec=pltpu.PrefetchScalarGridSpec(
            num_scalar_prefetch=2,
            grid=(panel,),
            in_specs=tile_specs(1),
            out_specs=pl.BlockSpec((CB, own_cols * CB), lambda g, *_: (g, 0)),
        ),
        out_shape=jax.ShapeDtypeStruct((width, own_cols * CB), jnp.bfloat16),
        compiler_params=params,
    )(row_tab, col_tab, arrived, arrived)

    group = 2
    lower = pl.pallas_call(
        functools.partial(lower_kernel, own_rows, own_cols, group, panel),
        grid_spec=pltpu.PrefetchScalarGridSpec(
            num_scalar_prefetch=3,
            grid=(own_rows // group,),
            in_specs=tile_specs(group) + [pl.BlockSpec((width, width), lambda g, *_: (0, 0))],
            out_specs=pl.BlockSpec((group * CB, width), lambda g, *_: (g, 0)),
            scratch_shapes=[pltpu.VMEM((group * CB, width), jnp.bfloat16)],
        ),
        out_shape=jax.ShapeDtypeStruct((own_rows * CB, width), jnp.bfloat16),
        compiler_params=params,
    )(row_tab, col_tab, place, *([arrived] * (2 * group)), diag_inverse)

    upper, lower = spread(upper, lower, n, m)

    return pl.pallas_call(
        functools.partial(final_kernel, own_rows, own_cols, group, panel, 4),
        grid_spec=pltpu.PrefetchScalarGridSpec(
            num_scalar_prefetch=4,
            grid=(own_rows // group,),
            in_specs=tile_specs(group)
            + [
                pl.BlockSpec((group * CB, width), lambda g, *_: (g, 0)),
                pl.BlockSpec((width, own_cols * CB), lambda g, *_: (0, 0)),
            ],
            out_specs=pl.BlockSpec((group * CB, own_cols * CB), lambda g, *_: (g, 0)),
        ),
        out_shape=jax.ShapeDtypeStruct((own_rows * CB, own_cols * CB), jnp.bfloat16),
        compiler_params=params,
    )(row_tab, col_tab, place, keep, *([arrived] * (2 * group)), lower, upper)


def solution(mesh):
    placed = (P("row", "col"), P(), P(), P())
    return jax.shard_map(
        body, mesh=mesh, in_specs=placed, out_specs=P("row", "col"), check_vma=False
    )
```

```python
import functools

import jax
import jax.numpy as jnp
from jax import lax
from jax.experimental import pallas as pl
from jax.experimental.pallas import tpu as pltpu
from jax.sharding import PartitionSpec as P

CB = 128
MESH = pl.DeviceIdType.MESH
VMEM_LIMIT = 56 * 1024 * 1024


def ranks(child_map, run, owned):
    count = child_map.shape[1]
    target = child_map // owned
    places = jnp.arange(count, dtype=jnp.int32)
    same = (target[:, :, None] == target[:, None, :]) & (
        (places[:, None] // run == places[None, :] // run) & (places[None, :] < places[:, None])
    )[None]
    return jnp.sum(same.astype(jnp.int32), axis=2)


def send_table(child_map, rank, child, start, run, owned, dests, cap):
    parents = lax.dynamic_slice(child_map, (child, start), (1, run))[0]
    rank = lax.dynamic_slice(rank, (child, start), (1, run))[0]
    slot = (parents // owned) * cap + rank
    hits = slot[None, :] == jnp.arange(dests * cap, dtype=jnp.int32)[:, None]
    return jnp.sum(jnp.where(hits, jnp.arange(run, dtype=jnp.int32)[None, :], 0), axis=1)


def receive_table(child_map, rank, mine, run, owned):
    count = child_map.shape[1]
    wanted = mine * owned + jnp.arange(owned, dtype=jnp.int32)
    hits = child_map[:, None, :] == wanted[None, :, None]
    shard = jnp.arange(count, dtype=jnp.int32) // run
    shard = jnp.sum(jnp.where(hits, shard[None, None, :], 0), axis=2)
    slot = jnp.sum(jnp.where(hits, rank[:, None, :], 0), axis=2)
    return shard, slot, jnp.any(hits, axis=2).astype(jnp.int32)


def pack_kernel(dests, slots, row_src, col_src, x0_ref, x1_ref, o_ref):
    for c in range(dests):
        for t in range(slots):
            at = pl.multiple_of(col_src[c * slots + t] * CB, CB)
            for i, x_ref in enumerate((x0_ref, x1_ref)):
                o_ref[0, c, i, :, t * CB : (t + 1) * CB] = x_ref[:, pl.ds(at, CB)]


def front_tile(tiles, flags, col_tab, own_cols, col):
    total = None
    for k in range(2):
        a = col_tab[(0 + k) * own_cols + col]
        t = pl.multiple_of(col_tab[(2 + k) * own_cols + col] * CB, CB)
        there = (flags[k] * col_tab[(4 + k) * own_cols + col]).astype(jnp.float32)
        there = jnp.full((CB, CB), there, jnp.float32).astype(jnp.bfloat16)
        part = tiles[k][0, a, 0, :, pl.ds(t, CB)] * there
        total = part if total is None else total + part
    return total


def row_flags(row_tab, own_rows, row):
    return [row_tab[(4 + k) * own_rows + row] for k in range(2)]


def upper_kernel(own_rows, own_cols, row_tab, col_tab, t0, t1, o_ref):
    flags = row_flags(row_tab, own_rows, pl.program_id(0))
    for j in range(own_cols):
        o_ref[:, j * CB : (j + 1) * CB] = front_tile((t0, t1), flags, col_tab, own_cols, j)


def lower_kernel(own_rows, own_cols, group, panel, row_tab, col_tab, place, *refs):
    tiles, (inv_ref, o_ref, held) = refs[: 2 * group], refs[2 * group :]
    for r in range(group):
        row = pl.program_id(0) * group + r
        flags = row_flags(row_tab, own_rows, row)
        for j in range(panel):
            held[r * CB : (r + 1) * CB, j * CB : (j + 1) * CB] = front_tile(
                tiles[2 * r : 2 * r + 2], flags, col_tab, own_cols, j
            )
    lower = jnp.dot(held[...], inv_ref[...], preferred_element_type=jnp.float32)
    for r in range(group):
        row = place[0] * own_rows + pl.program_id(0) * group + r
        below = (row >= panel).astype(jnp.float32)
        o_ref[r * CB : (r + 1) * CB, :] = (lower[r * CB : (r + 1) * CB] * below).astype(jnp.bfloat16)


def final_kernel(own_rows, own_cols, group, panel, wide, row_tab, col_tab, place, keep, *refs):
    tiles, (lower_ref, upper_ref, o_ref) = refs[: 2 * group], refs[2 * group :]
    rows = [pl.program_id(0) * group + r for r in range(group)]
    flags = [row_flags(row_tab, own_rows, row) for row in rows]

    def step(n, carry):
        at = n * (wide * CB)
        update = jnp.dot(
            lower_ref[...], upper_ref[:, pl.ds(at, wide * CB)], preferred_element_type=jnp.float32
        )
        for q in range(wide):
            col = n * wide + q
            for r in range(group):
                front = front_tile(tiles[2 * r : 2 * r + 2], flags[r], col_tab, own_cols, col)
                mask = keep[rows[r] * own_cols + col].astype(jnp.float32)
                part = update[r * CB : (r + 1) * CB, q * CB : (q + 1) * CB] * mask
                o_ref[r * CB : (r + 1) * CB, pl.ds(at + q * CB, CB)] = (
                    front.astype(jnp.float32) - part
                ).astype(jnp.bfloat16)
        return carry

    for n in range(own_cols // wide):
        step(n, 0)
    for r in range(group):

        @pl.when((place[1] == 0) & (place[0] * own_rows + rows[r] >= panel))
        def _():
            o_ref[r * CB : (r + 1) * CB, : panel * CB] = lower_ref[r * CB : (r + 1) * CB, :]


def spread_kernel(n, m, chunks, u_in, l_in, upper, lower, down, across, first, line, other, up, l_send, l_recv):
    row, col = lax.axis_index("row"), lax.axis_index("col")
    high, low = row // 2, row % 2
    barrier = pltpu.get_barrier_semaphore()
    for off in range(1, n):
        pl.semaphore_signal(barrier, inc=1, device_id=(lax.rem(row + off, n), col), device_id_type=MESH)
    for off in range(1, m):
        pl.semaphore_signal(barrier, inc=1, device_id=(row, lax.rem(col + off, m)), device_id_type=MESH)
    pl.semaphore_wait(barrier, n + m - 2)

    depth = upper.shape[0] // (2 * chunks)
    root = row == 0
    partner = high * 2 + (1 - low)
    goes_down = row + 2 < n
    goes_across = (row != 1) & (row != 0)
    goes_up = row == 3

    def move(half, c, send, recv, to):
        at = pl.multiple_of((half * chunks + c) * depth, depth)
        part = upper.at[pl.ds(at, depth), :]
        return pltpu.make_async_remote_copy(
            src_ref=part, dst_ref=part, send_sem=send.at[c], recv_sem=recv.at[c],
            device_id=(to, col), device_id_type=MESH,
        )

    def move_lower(p):
        return pltpu.make_async_remote_copy(
            src_ref=lower, dst_ref=lower, send_sem=l_send.at[p - 1], recv_sem=l_recv,
            device_id=(row, p), device_id_type=MESH,
        )

    for p in range(m - 1, 0, -1):

        @pl.when(col == 0)
        def _():
            move_lower(p).start()

    def lift(c):
        move(0, c, across, other, partner).wait_recv()
        move(0, c, up, other, 1).start()

    def send(c, carry):
        @pl.when(row != 0)
        def _():
            move(low, c, down, line, partner).wait_recv()

        @pl.when(goes_down)
        def _():
            move(low, c, down, line, row + 2).start()

        @pl.when(root)
        def _():
            move(1, c, first, line, 1).start()

        @pl.when(goes_across)
        def _():
            move(low, c, across, other, partner).start()

        @pl.when(goes_up & (c > 0))
        def _():
            lift(c - 1)

        return carry

    lax.fori_loop(0, chunks, send, 0)

    @pl.when(goes_up)
    def _():
        lift(chunks - 1)

    def finish(c, carry):
        @pl.when((row != 0) & jnp.logical_not(goes_up))
        def _():
            move(1 - low, c, across, other, partner).wait_recv()

        @pl.when(goes_up)
        def _():
            move(0, c, up, other, 1).wait_send()

        @pl.when(goes_down)
        def _():
            move(low, c, down, line, row + 2).wait_send()

        @pl.when(root)
        def _():
            move(1, c, first, line, 1).wait_send()

        @pl.when(goes_across)
        def _():
            move(low, c, across, other, partner).wait_send()

        return carry

    lax.fori_loop(0, chunks, finish, 0)

    @pl.when(col != 0)
    def _():
        move_lower(1).wait_recv()

    for p in range(1, m):

        @pl.when(col == 0)
        def _():
            move_lower(p).wait_send()


def spread(upper, lower, n, m):
    chunks = 24
    dma = pltpu.SemaphoreType.DMA
    anywhere = pl.BlockSpec(memory_space=pl.ANY)
    return pl.pallas_call(
        functools.partial(spread_kernel, n, m, chunks),
        out_shape=(
            jax.ShapeDtypeStruct(upper.shape, upper.dtype),
            jax.ShapeDtypeStruct(lower.shape, lower.dtype),
        ),
        in_specs=[anywhere] * 2,
        out_specs=(anywhere, anywhere),
        scratch_shapes=[dma((chunks,))] * 6 + [dma((m - 1,)), dma],
        input_output_aliases={0: 0, 1: 1},
        compiler_params=pltpu.CompilerParams(collective_id=0, has_side_effects=True),
    )(upper, lower)


def body(child_update, child_map, tile_mask, diag_inverse):
    n, m = lax.axis_size("row"), lax.axis_size("col")
    row_index, col_index = lax.axis_index("row"), lax.axis_index("col")
    per_child = n // 2
    blocks = child_map.shape[1]
    row_blocks, col_blocks = child_update.shape[0] // CB, child_update.shape[1] // CB
    own_rows, own_cols = tile_mask.shape[0] // n, tile_mask.shape[1] // m
    width = diag_inverse.shape[0]
    panel = width // CB
    cap_rows = 2 * (16 // n) * max(1, 8 // n)
    cap_cols = blocks // (m * m)
    child, within = row_index // per_child, row_index % per_child

    row_rank = ranks(child_map, row_blocks, own_rows)
    col_rank = ranks(child_map, col_blocks, own_cols)
    row_src = send_table(child_map, row_rank, child, within * row_blocks, row_blocks, own_rows, n, cap_rows)
    col_src = send_table(child_map, col_rank, child, col_index * col_blocks, col_blocks, own_cols, m, cap_cols)
    shard, slot, there = receive_table(child_map, row_rank, row_index, row_blocks, own_rows)
    shard = shard + per_child * jnp.arange(2, dtype=jnp.int32)[:, None]
    row_tab = jnp.concatenate([shard, slot, there]).reshape(-1)
    col_tab = jnp.concatenate(receive_table(child_map, col_rank, col_index, col_blocks, own_cols)).reshape(-1)
    place = jnp.stack([row_index, col_index]).astype(jnp.int32)
    keep = lax.dynamic_slice(
        tile_mask, (row_index * own_rows, col_index * own_cols), (own_rows, own_cols)
    ).reshape(-1)

    params = pltpu.CompilerParams(vmem_limit_bytes=VMEM_LIMIT)
    tile_block = (1, m, 1, CB, cap_cols * CB)
    packed = pl.pallas_call(
        functools.partial(pack_kernel, m, cap_cols),
        grid_spec=pltpu.PrefetchScalarGridSpec(
            num_scalar_prefetch=2,
            grid=(n * cap_rows // 2,),
            in_specs=[
                pl.BlockSpec((CB, col_blocks * CB), lambda g, rs, cs: (rs[2 * g], 0)),
                pl.BlockSpec((CB, col_blocks * CB), lambda g, rs, cs: (rs[2 * g + 1], 0)),
            ],
            out_specs=pl.BlockSpec(
                (1, m, 2, CB, cap_cols * CB),
                lambda g, rs, cs: (g // (cap_rows // 2), 0, g % (cap_rows // 2), 0, 0),
            ),
        ),
        out_shape=jax.ShapeDtypeStruct((n, m, cap_rows, CB, cap_cols * CB), jnp.bfloat16),
        compiler_params=params,
    )(row_src, col_src, child_update, child_update)
    arrived = lax.all_to_all(
        packed.reshape(n * m, cap_rows, CB, cap_cols * CB), ("row", "col"), split_axis=0, concat_axis=0, tiled=True
    ).reshape(packed.shape)

    def tile_specs(group):
        def spec(r, k):
            def where(g, row_tab, *_):
                row = g * group + r
                return (row_tab[k * own_rows + row], 0, row_tab[(2 + k) * own_rows + row], 0, 0)

            return pl.BlockSpec(tile_block, where)

        return [spec(r, k) for r in range(group) for k in range(2)]

    upper = pl.pallas_call(
        functools.partial(upper_kernel, own_rows, own_cols),
        grid_spec=pltpu.PrefetchScalarGridSpec(
            num_scalar_prefetch=2,
            grid=(panel,),
            in_specs=tile_specs(1),
            out_specs=pl.BlockSpec((CB, own_cols * CB), lambda g, *_: (g, 0)),
        ),
        out_shape=jax.ShapeDtypeStruct((width, own_cols * CB), jnp.bfloat16),
        compiler_params=params,
    )(row_tab, col_tab, arrived, arrived)

    group = 4
    lower = pl.pallas_call(
        functools.partial(lower_kernel, own_rows, own_cols, group, panel),
        grid_spec=pltpu.PrefetchScalarGridSpec(
            num_scalar_prefetch=3,
            grid=(own_rows // group,),
            in_specs=tile_specs(group) + [pl.BlockSpec((width, width), lambda g, *_: (0, 0))],
            out_specs=pl.BlockSpec((group * CB, width), lambda g, *_: (g, 0)),
            scratch_shapes=[pltpu.VMEM((group * CB, width), jnp.bfloat16)],
        ),
        out_shape=jax.ShapeDtypeStruct((own_rows * CB, width), jnp.bfloat16),
        compiler_params=params,
    )(row_tab, col_tab, place, *([arrived] * (2 * group)), diag_inverse)

    upper, lower = spread(upper, lower, n, m)

    return pl.pallas_call(
        functools.partial(final_kernel, own_rows, own_cols, group, panel, 4),
        grid_spec=pltpu.PrefetchScalarGridSpec(
            num_scalar_prefetch=4,
            grid=(own_rows // group,),
            in_specs=tile_specs(group)
            + [
                pl.BlockSpec((group * CB, width), lambda g, *_: (g, 0)),
                pl.BlockSpec((width, own_cols * CB), lambda g, *_: (0, 0)),
            ],
            out_specs=pl.BlockSpec((group * CB, own_cols * CB), lambda g, *_: (g, 0)),
        ),
        out_shape=jax.ShapeDtypeStruct((own_rows * CB, own_cols * CB), jnp.bfloat16),
        compiler_params=params,
    )(row_tab, col_tab, place, keep, *([arrived] * (2 * group)), lower, upper)


def solution(mesh):
    placed = (P("row", "col"), P(), P(), P())
    return jax.shard_map(
        body, mesh=mesh, in_specs=placed, out_specs=P("row", "col"), check_vma=False
    )
```
